32 devices in a mesh: seq: 16 (over z, y, x), head: 2 (over core).
Axes of the slice: x: 2, y: 2, z: 4, core: 2. Of those that a mesh axis runs over, the one named last changes fastest.
Arguments:
- byte_states: bfloat16 [16384, 1024], P('seq'), may hold values from -8 to 8
- doc_ids: int32 [16384], P('seq'), may hold values from 0 to 31, never falling along the last dimension, each value on 1 to 2048 neighbouring positions
- boundary_flags: int32 [16384], P('seq'), may hold values from 0 to 1, as said below
- w_qkv: bfloat16 [3, 1024, 1024], P(None, None, 'head'), may hold values from -0.22097087 to 0.22097087
- w_out: bfloat16 [1024, 1024], P('head'), may hold values from -0.375 to 0.375
- w_span: bfloat16 [1024, 2048], replicated, may hold values from -0.1875 to 0.1875
- w_gate: bfloat16 [2048, 4608], P('seq', 'head'), may hold values from -0.125 to 0.125
- w_up: bfloat16 [2048, 4608], P('seq', 'head'), may hold values from -0.125 to 0.125
- w_down: bfloat16 [4608, 2048], P('head', 'seq'), may hold values from -0.09375 to 0.09375
- w_back: bfloat16 [2048, 1024], replicated, may hold values from -0.125 to 0.125
Outputs:
- byte_out: bfloat16 [16384, 1024], P('seq')
The draws below stay inside these ranges and needn't reach their ends.
Inputs may be any that keep to these rules, and one draw needn't show every extreme that they name: `boundary_flags`: byte 0 starts a group. Each aligned block of 1024 bytes holds between 128 and 512 group starts, and some block holds exactly 512. In every block but the first, its first 256 bytes start no group. `doc_ids`: never falling; each document has 1 to 2048 bytes, one exactly 2048.
All inputs are finite; a program needn't handle non-finite values.
Results may differ from the reference program's by a relative error of at most 0.012.
The reference program's roundings to bfloat16 on the way count: a program that leaves them out, or rounds other values in their place, can miss the bound.
Values may be sent and summed in bfloat16 or wider, within the bound.
A program may use at most 128 MiB of HBM per device.

```python
import math
import jax
import jax.numpy as jnp
import numpy as np
from jax import lax

DB = 1024
HD = 128
DM = 2048
FF = 4608
WIN = 1024
TOK_DEV = 1024
CAP = 512
BYTES = 16384
N_SEQ = 16


def draw_byte_states(key, part):
    key = jax.random.fold_in(key, 21)
    noise_key = jax.random.fold_in(key, 0)
    noise = jax.random.normal(noise_key, (BYTES, DB), jnp.float32)
    result = jnp.clip(noise, -6.0, 6.0)
    return result.astype(jnp.bfloat16)


def draw_w_qkv(key, part):
    key = jax.random.fold_in(key, 22)
    base_key = jax.random.fold_in(key, 0)
    gains = jnp.array([2.0 ** 0.5, 2.0 ** 0.5, 1.0], jnp.float32)[:, None, None] * DB ** (-0.5)
    raw = jax.random.normal(base_key, (3, DB, DB), jnp.float32)
    result = jnp.clip(raw, -5.0, 5.0) * gains
    return result.astype(jnp.bfloat16)


def draw_boundary_flags(key, part):
    key = jax.random.fold_in(key, 11)
    shards = BYTES // TOK_DEV
    quiet = TOK_DEV // 4
    rest = TOK_DEV - quiet
    count_key, pick_key, order_key = jax.random.split(key, 3)
    counts = jax.random.randint(count_key, (shards,), CAP // 4, CAP + 1)
    busiest = jax.random.randint(pick_key, (), 0, shards)
    counts = jnp.where(jnp.arange(shards) == busiest, CAP, counts)
    shard_keys = jax.random.split(order_key, shards)

    def one_order(single):
        return jax.random.permutation(single, rest)
    orders = jax.vmap(one_order)(shard_keys)
    ranks = jnp.argsort(orders, axis=1).astype(jnp.int32)
    limits = counts.at[0].add(-1)
    tail_flags = (ranks < limits[:, None]).astype(jnp.int32)
    flags = jnp.concatenate([jnp.zeros((shards, quiet), jnp.int32), tail_flags], axis=1)
    flags = flags.at[0, 0].set(1)
    return flags.reshape(BYTES)


def block_levels(stream_key, dims, cuts, smallest, top_value):
    def one(axis_at, shards_of):
        heights = jax.random.uniform(jax.random.fold_in(jax.random.fold_in(stream_key, 6), axis_at), (shards_of,), jnp.float32, smallest / len(cuts), top_value / len(cuts))
        return jnp.repeat(jnp.exp(heights), dims[axis_at] // shards_of).reshape((-1,) + (1,) * (len(dims) - axis_at - 1))

    level = one(*cuts[0])
    for cut in cuts[1:]:
        level = level * one(*cut)
    return level


def length_profile(number_of, total, most, skew):
    weights = [(1 << 20) // math.isqrt(grade ** skew) + 1 for grade in range(2, number_of + 1)]
    spare, holding = total - most - (number_of - 1), [1] * (number_of - 1)
    while spare > 0:
        free = [i for i in range(number_of - 1) if holding[i] < most]
        whole, remaining = sum([weights[i] for i in free]), spare
        for i in free:
            more = min(most - holding[i], max(1, remaining * weights[i] // whole), spare)
            holding[i] = holding[i] + more
            spare = spare - more
    return np.array([most] + holding)


def ragged(stream_key, count, total, reach, slope):
    if count == 2:
        one = jax.random.randint(stream_key, (), max(1, total - reach), min(reach, total - 1) + 1)
        return jnp.stack([one, total - one])
    tallies = jnp.asarray(length_profile(count, total, reach, slope), jnp.int32)
    couples = (count - 1) // 2
    giver, receiver = tallies[1:1 + 2 * couples:2], tallies[2:2 + 2 * couples:2]
    margin = jnp.minimum(giver - 1, reach - receiver)
    moved = jax.random.randint(jax.random.fold_in(stream_key, 1), (couples,), 0, 1 << 20) % (margin + 1)
    tallies = tallies.at[1:1 + 2 * couples:2].set(giver - moved).at[2:2 + 2 * couples:2].set(receiver + moved)
    return tallies[jax.random.permutation(jax.random.fold_in(stream_key, 2), count)]


def gaussian(rng, shape, scale, limit, cuts=(), kind=jnp.bfloat16):
    factor_of = block_levels(rng, shape, cuts, -0.22, 0.18) if cuts else 1.0
    values = jax.random.normal(rng, shape, jnp.float32) * scale * factor_of
    return jnp.minimum(jnp.maximum(values, -limit), limit).astype(kind)


def setup_inputs(seed: int = 0) -> dict:
    seeds = jax.random.split(jax.random.key(seed), 11)
    return {
        "byte_states": draw_byte_states(jax.random.fold_in(seeds[10], 71), 0),
        "doc_ids": jnp.searchsorted(jnp.cumsum(ragged(seeds[1], BYTES // (WIN // 2), BYTES, 2 * WIN, 1)), jnp.arange(BYTES), side="right").astype(jnp.int32),
        "boundary_flags": draw_boundary_flags(jax.random.fold_in(seeds[10], 71), 0),
        "w_qkv": draw_w_qkv(jax.random.fold_in(seeds[10], 71), 0),
        "w_out": gaussian(seeds[4], (DB, DB), (DB // 4) ** -0.5, 0.375, ((0, 2),)),
        "w_span": gaussian(seeds[5], (DB, DM), DB ** -0.5, 0.1875),
        "w_gate": gaussian(seeds[6], (DM, FF), DM ** -0.5, 0.125, ((0, 16), (1, 2))),
        "w_up": gaussian(seeds[7], (DM, FF), DM ** -0.5, 0.125, ((0, 16), (1, 2))),
        "w_down": gaussian(seeds[8], (FF, DM), FF ** -0.5, 0.09375, ((0, 2), (1, 16))),
        "w_back": gaussian(seeds[9], (DM, DB), DM ** -0.5, 0.125),
    }


eps = 1e-06

def rms_rows(values):
    mean_sq = lax.optimization_barrier(jnp.mean(values * values, axis=-1, keepdims=True))
    return values * lax.rsqrt(mean_sq + eps)

def reference(byte_states, doc_ids, boundary_flags, w_qkv, w_out, w_span, w_gate, w_up, w_down, w_back):
    total = byte_states.shape[0]
    heads = DB // HD
    normed = rms_rows(byte_states.astype(jnp.float32)).astype(jnp.bfloat16)
    queries = jnp.dot(normed, w_qkv[0], preferred_element_type=jnp.float32).astype(jnp.bfloat16)
    keys = jnp.dot(normed, w_qkv[1], preferred_element_type=jnp.float32).astype(jnp.bfloat16)
    values = jnp.dot(normed, w_qkv[2], preferred_element_type=jnp.float32).astype(jnp.bfloat16)
    block = min(512, TOK_DEV)
    padded_keys = jnp.pad(keys, ((WIN, 0), (0, 0)))
    padded_values = jnp.pad(values, ((WIN, 0), (0, 0)))
    padded_docs = jnp.pad(doc_ids, (WIN, 0), constant_values=-1)
    scale = 1.0 / HD ** 0.5

    def one_block(index):
        start = (index * block).astype(jnp.int32)
        q_blk = lax.dynamic_slice_in_dim(queries, start, block, 0)
        k_blk = lax.dynamic_slice_in_dim(padded_keys, start, WIN + block, 0)
        v_blk = lax.dynamic_slice_in_dim(padded_values, start, WIN + block, 0)
        q_docs = lax.dynamic_slice_in_dim(doc_ids, start, block, 0)
        k_docs = lax.dynamic_slice_in_dim(padded_docs, start, WIN + block, 0)
        distance = jnp.arange(block)[:, None] - (jnp.arange(WIN + block)[None, :] - WIN)
        allowed = (distance >= 0) & (distance < WIN) & (q_docs[:, None] == k_docs[None, :])
        q_four = q_blk.reshape(block, heads, HD).astype(jnp.float32)
        k_four = k_blk.reshape(WIN + block, heads, HD).astype(jnp.float32)
        v_four = v_blk.reshape(WIN + block, heads, HD).astype(jnp.float32)
        scores = jnp.einsum('qhd,khd->hqk', q_four, k_four) * scale
        scores = jnp.where(allowed[None], scores, -1e+30)
        top = lax.optimization_barrier(jnp.max(scores, axis=-1, keepdims=True))
        expo = jnp.exp(scores - top)
        probs = expo / lax.optimization_barrier(jnp.sum(expo, axis=-1, keepdims=True))
        weights = probs.astype(jnp.bfloat16).astype(jnp.float32)
        mixed = jnp.einsum('hqk,khd->qhd', weights, v_four)
        return mixed.reshape(block, DB).astype(jnp.bfloat16)
    attended = lax.map(one_block, jnp.arange(total // block)).reshape(total, DB)
    term = jnp.dot(attended, w_out, preferred_element_type=jnp.float32)
    encoded = (byte_states.astype(jnp.float32) + term).astype(jnp.bfloat16)
    group = jnp.cumsum(boundary_flags, dtype=jnp.int32) - 1
    slot_count = N_SEQ * CAP
    sums = jax.ops.segment_sum(encoded.astype(jnp.float32), group, num_segments=slot_count)
    counts = jax.ops.segment_sum(jnp.ones((total,), jnp.float32), group, num_segments=slot_count)
    pooled = (sums / jnp.maximum(counts, 1.0)[:, None]).astype(jnp.bfloat16)
    group_in = jnp.dot(pooled, w_span, preferred_element_type=jnp.float32).astype(jnp.bfloat16)
    group_normed = rms_rows(group_in.astype(jnp.float32)).astype(jnp.bfloat16)
    gate = jnp.dot(group_normed, w_gate, preferred_element_type=jnp.float32)
    up = jnp.dot(group_normed, w_up, preferred_element_type=jnp.float32)
    hidden = (jax.nn.silu(gate) * up).astype(jnp.bfloat16)
    main = (group_in.astype(jnp.float32) + jnp.dot(hidden, w_down, preferred_element_type=jnp.float32)).astype(jnp.bfloat16)
    back = jnp.dot(main, w_back, preferred_element_type=jnp.float32).astype(jnp.bfloat16)
    before = group - 1
    lifted = jnp.take(back, jnp.maximum(before, 0).astype(jnp.int32), axis=0).astype(jnp.float32)
    lifted = jnp.where((before >= 0)[:, None], lifted, jnp.float32(0.0))
    return (encoded.astype(jnp.float32) + lifted).astype(jnp.bfloat16)
```

```python
import functools

import jax
import jax.numpy as jnp
from jax import lax
from jax.experimental import pallas as pl
from jax.experimental.pallas import tpu as pltpu
from jax.sharding import PartitionSpec as P

HD = 128
WIN = 1024
CAP = 512
QB = 256
PAIR = 4

eps = 1e-06
f32 = jnp.float32
bf16 = jnp.bfloat16
VM = pl.BlockSpec(memory_space=pltpu.VMEM)
ANY = pl.BlockSpec(memory_space=pl.ANY)
MIB = 1 << 20


def shifted(block, axis, distance):
    devices = range(lax.axis_size(axis))
    route = [(i - distance, i) for i in devices if i - distance in devices]
    return lax.ppermute(block, axis, route)


def swapped(block, bit, axis="seq"):
    return lax.ppermute(block, axis, [(i, i ^ bit) for i in range(lax.axis_size(axis))])


def flip(number, bit):
    return number + bit - 2 * bit * ((number // bit) % 2)


def params(mib=48):
    return pltpu.CompilerParams(vmem_limit_bytes=mib * MIB)


def cost(flops, moved):
    return pl.CostEstimate(flops=int(flops), bytes_accessed=int(moved), transcendentals=0)


def rms_rows(values):
    mean_sq = jnp.mean(values * values, axis=-1, keepdims=True)
    return values * lax.rsqrt(mean_sq + eps)


def attend_kernel(qd_ref, kd_ref, q_ref, pk_ref, k_ref, pv_ref, v_ref, o_ref, bias):
    rows = q_ref.shape[0]
    span = WIN + QB

    @pl.when(pl.program_id(0) == 0)
    def _():
        for i in range(rows // QB):
            far = lax.broadcasted_iota(jnp.int32, (QB, span), 0) - (
                lax.broadcasted_iota(jnp.int32, (QB, span), 1) - WIN
            )
            same = qd_ref[i * QB : (i + 1) * QB, :] == kd_ref[:, i * QB : i * QB + span]
            allowed = (far >= 0) & (far < WIN) & same
            bias[i] = jnp.where(allowed, 0.0, -1e30).astype(f32)

    scale = 1.0 / HD**0.5
    nt = (((1,), (1,)), ((), ()))
    for i in range(rows // QB):
        first = i * QB
        cut = WIN - first
        q = q_ref[first : first + QB, :]
        own = first + QB
        s_a = lax.dot_general(q, pk_ref[first:, :], nt, preferred_element_type=f32)
        s_b = lax.dot_general(q, k_ref[:own, :], nt, preferred_element_type=f32)
        s_a = s_a * scale + bias[i, :, :cut]
        s_b = s_b * scale + bias[i, :, cut:]
        top = jnp.maximum(
            jnp.max(s_a, axis=-1, keepdims=True), jnp.max(s_b, axis=-1, keepdims=True)
        )
        e_a = jnp.exp(s_a - top)
        e_b = jnp.exp(s_b - top)
        inv = 1.0 / (
            jnp.sum(e_a, axis=-1, keepdims=True) + jnp.sum(e_b, axis=-1, keepdims=True)
        )
        mixed = jnp.dot((e_a * inv).astype(bf16), pv_ref[first:, :], preferred_element_type=f32)
        mixed += jnp.dot((e_b * inv).astype(bf16), v_ref[:own, :], preferred_element_type=f32)
        o_ref[first : first + QB, :] = mixed.astype(bf16)


def attend(q_docs, k_docs, q, pk, k, pv, v):
    rows, width = q.shape
    col = pl.BlockSpec((rows, HD), lambda h: (0, h))
    return pl.pallas_call(
        attend_kernel,
        grid=(width // HD,),
        in_specs=[
            pl.BlockSpec((rows, 1), lambda h: (0, 0)),
            pl.BlockSpec((1, rows + WIN), lambda h: (0, 0)),
            col, col, col, col, col,
        ],
        out_specs=col,
        out_shape=jax.ShapeDtypeStruct((rows, width), bf16),
        scratch_shapes=[pltpu.VMEM((rows // QB, QB, WIN + QB), f32)],
        compiler_params=params(),
        cost_estimate=cost(16e9, 6 * MIB),
    )(q_docs, k_docs, q, pk, k, pv, v)


def pool_kernel(mine, other, w_mine, w_other, bytes_ref, ids, enc, sums, lead):
    half = bytes_ref.shape[0] // 2
    for i in range(2):
        part = slice(i * half, (i + 1) * half)
        term = jnp.dot(mine[part, :], w_mine[...], preferred_element_type=f32)
        term += jnp.dot(other[part, :], w_other[...], preferred_element_type=f32)
        enc[part, :] = (bytes_ref[part, :].astype(f32) + term).astype(bf16)
    rows = bytes_ref.shape[0]
    slot = lax.broadcasted_iota(jnp.int32, (CAP, rows), 0)
    member = (ids[...] == slot).astype(f32).astype(bf16)
    sums[...] = jnp.dot(member, enc[...], preferred_element_type=f32)
    leading = jnp.broadcast_to((ids[...] < 0).astype(f32), (8, rows))
    count = jnp.sum(leading, axis=1, keepdims=True)
    total = jnp.dot(leading.astype(bf16), enc[...], preferred_element_type=f32)
    at = lax.broadcasted_iota(jnp.int32, total.shape, 0)
    lead[...] = jnp.where(at == 1, count, total)


def pool(mine, other, w_mine, w_other, byte_states, ids_row):
    rows, width = byte_states.shape
    return pl.pallas_call(
        pool_kernel,
        in_specs=[VM] * 6,
        out_specs=[VM] * 3,
        out_shape=[
            jax.ShapeDtypeStruct((rows, width), bf16),
            jax.ShapeDtypeStruct((CAP, width), f32),
            jax.ShapeDtypeStruct((8, width), f32),
        ],
        compiler_params=params(),
        cost_estimate=cost(4e9, 10 * MIB),
    )(mine, other, w_mine, w_other, byte_states, ids_row)


def main_kernel(n_pairs, sources, gn, *refs):
    gus, dns = refs[:n_pairs], refs[n_pairs : 2 * n_pairs]
    keep, send, wg, wu, wd, hid, sem_g, sem_u, sem_d = refs[2 * n_pairs :]
    depth = wg.shape[0] // (2 * n_pairs)
    s = lax.axis_index("seq")
    h = lax.axis_index("head")
    copies_g, copies_u, copies_d = [], [], []
    for j in range(n_pairs):
        for m in range(2):
            if sources is None:
                place = (2 * j + m) * depth
            else:
                index = s
                for bit in sources[j][m]:
                    index = flip(index, bit)
                place = pl.multiple_of(index * depth, depth)
            rows = pl.ds(m * depth, depth)
            at = 2 * j + m
            copies_g.append(pltpu.make_async_copy(
                gus[j].at[0, rows], wg.at[pl.ds(place, depth)], sem_g.at[at]))
            copies_u.append(pltpu.make_async_copy(
                gus[j].at[1, rows], wu.at[pl.ds(place, depth)], sem_u.at[at]))
            copies_d.append(pltpu.make_async_copy(
                dns[j].at[m], wd.at[:, pl.ds(place, depth)], sem_d.at[at]))
    for copy in copies_g + copies_u + copies_d:
        copy.start()
    for copy in copies_g + copies_u:
        copy.wait()
    units = wg.shape[1]
    tile = 384
    for t in range(units // tile):
        cols = slice(t * tile, (t + 1) * tile)
        gate = jnp.dot(gn[...], wg[:, cols], preferred_element_type=f32)
        up = jnp.dot(gn[...], wu[:, cols], preferred_element_type=f32)
        hid[:, cols] = (jax.nn.silu(gate) * up).astype(bf16)
    for copy in copies_d:
        copy.wait()
    width = send.shape[1]
    step = 512
    for t in range(width // step):
        out = pl.ds(t * step, step)
        there = pl.ds(pl.multiple_of((1 - h) * width + t * step, step), step)
        send[:, out] = jnp.dot(hid[...], wd[:, there], preferred_element_type=f32).astype(bf16)
    for t in range(width // step):
        out = pl.ds(t * step, step)
        here = pl.ds(pl.multiple_of(h * width + t * step, step), step)
        keep[:, out] = jnp.dot(hid[...], wd[:, here], preferred_element_type=f32)


def main_layer(gn, gus, dns, sources):
    tokens, dm = gn.shape
    units = gus[0].shape[2]
    n_pairs = len(gus)
    n_blocks = 2 * n_pairs
    return pl.pallas_call(
        functools.partial(main_kernel, n_pairs, sources),
        in_specs=[VM] + [ANY] * (2 * n_pairs),
        out_specs=[VM, VM],
        out_shape=[
            jax.ShapeDtypeStruct((tokens, dm // 2), f32),
            jax.ShapeDtypeStruct((tokens, dm // 2), bf16),
        ],
        scratch_shapes=[
            pltpu.VMEM((dm, units), bf16),
            pltpu.VMEM((dm, units), bf16),
            pltpu.VMEM((units, dm), bf16),
            pltpu.VMEM((tokens, units), bf16),
            pltpu.SemaphoreType.DMA((n_blocks,)),
            pltpu.SemaphoreType.DMA((n_blocks,)),
            pltpu.SemaphoreType.DMA((n_blocks,)),
        ],
        compiler_params=params(),
        cost_estimate=cost(8e9, 20 * MIB),
    )(gn, *gus, *dns)


def back_kernel(starts, mine, other, w_back, back, tail):
    h = lax.axis_index("head")
    half = mine.shape[1]
    w_mine = w_back[pl.ds(pl.multiple_of(h * half, half), half), :]
    w_other = w_back[pl.ds(pl.multiple_of((1 - h) * half, half), half), :]
    total = jnp.dot(mine[...], w_mine, preferred_element_type=f32)
    total += jnp.dot(other[...], w_other, preferred_element_type=f32)
    back[...] = total.astype(bf16)
    row = lax.broadcasted_iota(jnp.int32, (16, CAP), 0)
    slot = lax.broadcasted_iota(jnp.int32, (16, CAP), 1)
    pick = (slot == starts[0] - 2 + row) & (row < 2)
    tail[...] = jnp.dot(
        pick.astype(f32).astype(bf16), back[...], preferred_element_type=f32
    ).astype(bf16)


def back_rows(starts, mine, other, w_back):
    width = w_back.shape[1]
    return pl.pallas_call(
        back_kernel,
        in_specs=[pl.BlockSpec(memory_space=pltpu.SMEM), VM, VM, VM],
        out_specs=[VM, VM],
        out_shape=[
            jax.ShapeDtypeStruct((mine.shape[0], width), bf16),
            jax.ShapeDtypeStruct((16, width), bf16),
        ],
        compiler_params=params(),
        cost_estimate=cost(3e9, 8 * MIB),
    )(starts, mine, other, w_back)


def lift_kernel(ids, enc, back, tail, out):
    group = ids[...]
    rows = group.shape[0]
    slot = lax.broadcasted_iota(jnp.int32, (rows, CAP), 1)
    pick = (group - 1 == slot).astype(f32).astype(bf16)
    lifted = jnp.dot(pick, back[...], preferred_element_type=f32)
    lifted += jnp.where(group == -1, tail[0:1, :].astype(f32), 0.0)
    lifted += jnp.where(group == 0, tail[1:2, :].astype(f32), 0.0)
    out[...] = (enc[...].astype(f32) + lifted).astype(bf16)


def lift(ids_col, encoded, back, tail):
    rows, width = encoded.shape
    block = 256
    return pl.pallas_call(
        lift_kernel,
        grid=(rows // block,),
        in_specs=[
            pl.BlockSpec((block, 1), lambda i: (i, 0)),
            pl.BlockSpec((block, width), lambda i: (i, 0)),
            pl.BlockSpec(back.shape, lambda i: (0, 0)),
            pl.BlockSpec(tail.shape, lambda i: (0, 0)),
        ],
        out_specs=pl.BlockSpec((block, width), lambda i: (i, 0)),
        out_shape=jax.ShapeDtypeStruct((rows, width), bf16),
        compiler_params=params(),
        cost_estimate=cost(2e9, 6 * MIB),
    )(ids_col, encoded, back, tail)


def gather_weights(w_gate, w_up, w_down, role):
    n_seq = lax.axis_size("seq")
    units = w_gate.shape[1] // 2
    depth = w_gate.shape[0]

    if n_seq != 16:
        mine = role * units
        gate = lax.dynamic_slice_in_dim(lax.all_gather(w_gate, "seq", axis=0, tiled=True), mine, units, 1)
        up = lax.dynamic_slice_in_dim(lax.all_gather(w_up, "seq", axis=0, tiled=True), mine, units, 1)
        down = lax.dynamic_slice_in_dim(lax.all_gather(w_down, "seq", axis=1, tiled=True), mine, units, 0)
        both = jnp.stack([gate, up])
        gus = [both[:, i : i + 256] for i in range(0, both.shape[1], 256)]
        dns = [
            jnp.stack([down[:, i : i + 128], down[:, i + 128 : i + 256]])
            for i in range(0, down.shape[1], 256)
        ]
        return gus, dns, None

    def half(of):
        return (
            jnp.stack([
                lax.dynamic_slice_in_dim(w_gate, of * units, units, 1),
                lax.dynamic_slice_in_dim(w_up, of * units, units, 1),
            ]),
            lax.dynamic_slice_in_dim(w_down, of * units, units, 0),
        )

    gu_mine, dn_mine = half(role)
    gu_theirs, dn_theirs = half(1 - role)
    gu = jnp.concatenate([gu_mine, swapped(gu_theirs, PAIR)], axis=1)
    dn = jnp.stack([dn_mine, swapped(dn_theirs, PAIR)])

    gu_z = swapped(gu, 8)
    gu_x, gu_y = swapped(gu, 1), swapped(gu, 2)
    dn_z = swapped(dn, 8)
    gu_xy = jnp.stack([swapped(gu_x[0], 2), swapped(gu_y[1], 1)])
    gu_zx, gu_zy = swapped(gu_z, 1), swapped(gu_z, 2)
    dn_x, dn_y = swapped(dn, 1), swapped(dn, 2)
    gu_zxy = jnp.stack([swapped(gu_zx[0], 2), swapped(gu_zy[1], 1)])
    dn_xy = swapped(dn_x, 2)
    dn_zx, dn_zy = swapped(dn_z, 1), swapped(dn_z, 2)
    dn_zxy = swapped(dn_zy, 1)
    gus = [gu, gu_z, gu_x, gu_y, gu_xy, gu_zx, gu_zy, gu_zxy]
    dns = [dn, dn_z, dn_x, dn_y, dn_xy, dn_zx, dn_zy, dn_zxy]
    ways = [(), (8,), (1,), (2,), (1, 2), (8, 1), (8, 2), (8, 1, 2)]
    sources = [(way, way + (PAIR,)) for way in ways]
    return gus, dns, sources


def by_head(mine, other, head, axis):
    low = jnp.where(head == 0, mine, other)
    high = jnp.where(head == 0, other, mine)
    return jnp.concatenate([low, high], axis=axis)


def body(byte_states, doc_ids, boundary_flags, w_qkv, w_out, w_span, w_gate, w_up, w_down, w_back):
    rows, width = byte_states.shape
    s = lax.axis_index("seq")
    head = lax.axis_index("head")
    role = (s // PAIR) % 2

    half = lax.dynamic_slice_in_dim(byte_states, head * (rows // 2), rows // 2, 0)
    prior_half = shifted(half, "seq", 1)
    prior_docs = jnp.where(s == 0, -1, shifted(doc_ids, "seq", 1))
    w_out_other = swapped(w_out, 1, "head")
    gus, dns, sources = gather_weights(w_gate, w_up, w_down, role)

    normed = rms_rows(byte_states.astype(f32)).astype(bf16)
    queries = jnp.dot(normed, w_qkv[0], preferred_element_type=f32).astype(bf16)
    keys = jnp.dot(normed, w_qkv[1], preferred_element_type=f32).astype(bf16)
    values = jnp.dot(normed, w_qkv[2], preferred_element_type=f32).astype(bf16)
    prior = by_head(prior_half, swapped(prior_half, 1, "head"), head, 0)
    prior_normed = rms_rows(prior.astype(f32)).astype(bf16)
    prior_keys = jnp.dot(prior_normed, w_qkv[1], preferred_element_type=f32).astype(bf16)
    prior_values = jnp.dot(prior_normed, w_qkv[2], preferred_element_type=f32).astype(bf16)

    all_docs = jnp.concatenate([prior_docs, doc_ids])
    attended = attend(
        doc_ids[:, None], all_docs[None, :], queries, prior_keys, keys, prior_values, values
    )
    attended_other = swapped(attended, 1, "head")

    local_ids = jnp.cumsum(boundary_flags, dtype=jnp.int32) - 1
    starts = jnp.sum(boundary_flags, dtype=jnp.int32)
    encoded, sums, lead = pool(
        attended, attended_other, w_out, w_out_other, byte_states, local_ids[None, :]
    )
    following = shifted(lead, "seq", -1)
    slots = jnp.arange(CAP, dtype=jnp.int32)
    counts = jnp.sum(local_ids[None, :] == slots[:, None], axis=1).astype(f32)
    last_slot = slots == starts - 1
    sums = sums + jnp.where(last_slot[:, None], following[0:1], f32(0.0))
    counts = counts + jnp.where(last_slot, following[1, 0], f32(0.0))
    pooled = (sums / jnp.maximum(counts, 1.0)[:, None]).astype(bf16)

    share = lax.dynamic_slice_in_dim(pooled, head * (width // 2), width // 2, 1)
    got = swapped(share, PAIR)
    pooled_partner = by_head(got, swapped(got, 1, "head"), head, 1)

    def enter(values):
        group_in = jnp.dot(values, w_span, preferred_element_type=f32).astype(bf16)
        return group_in, rms_rows(group_in.astype(f32)).astype(bf16)

    group_in, group_normed = enter(pooled)
    _, partner_normed = enter(pooled_partner)
    keep_p, send_p = main_layer(partner_normed, gus, dns, sources)
    partner_sum = (keep_p + swapped(send_p, 1, "head").astype(f32)).astype(bf16)
    from_partner = swapped(partner_sum, PAIR)
    keep, send = main_layer(group_normed, gus, dns, sources)
    own_sum = keep + swapped(send, 1, "head").astype(f32)
    dm_half = keep.shape[1]
    in_half = lax.dynamic_slice_in_dim(group_in, head * dm_half, dm_half, 1)
    main = (in_half.astype(f32) + own_sum + from_partner.astype(f32)).astype(bf16)
    main_other = swapped(main, 1, "head")
    back, tail = back_rows(starts[None], main, main_other, w_back)
    prior_tail = shifted(tail, "seq", 1)
    return lift(local_ids[:, None], encoded, back, prior_tail)


def solution(mesh):
    placed = (
        P("seq", None),
        P("seq"),
        P("seq"),
        P(None, None, "head"),
        P("head", None),
        P(),
        P("seq", "head"),
        P("seq", "head"),
        P("head", "seq"),
        P(),
    )
    return jax.shard_map(
        body, mesh=mesh, in_specs=placed, out_specs=P("seq", None), check_vma=False
    )
```

```python
import functools

import jax
import jax.numpy as jnp
from jax import lax
from jax.experimental import pallas as pl
from jax.experimental.pallas import tpu as pltpu
from jax.sharding import PartitionSpec as P

HD = 128
WIN = 1024
CAP = 512
QB = 256
PAIR = 4

eps = 1e-06
f32 = jnp.float32
bf16 = jnp.bfloat16
VM = pl.BlockSpec(memory_space=pltpu.VMEM)
ANY = pl.BlockSpec(memory_space=pl.ANY)
MIB = 1 << 20


def shifted(block, axis, distance):
    devices = range(lax.axis_size(axis))
    route = [(i - distance, i) for i in devices if i - distance in devices]
    return lax.ppermute(block, axis, route)


def swapped(block, bit, axis="seq"):
    return lax.ppermute(block, axis, [(i, i ^ bit) for i in range(lax.axis_size(axis))])


def flip(number, bit):
    return number + bit - 2 * bit * ((number // bit) % 2)


def params(mib=48):
    return pltpu.CompilerParams(vmem_limit_bytes=mib * MIB)


def cost(flops, moved):
    return pl.CostEstimate(flops=int(flops), bytes_accessed=int(moved), transcendentals=0)


def rms_rows(values):
    mean_sq = jnp.mean(values * values, axis=-1, keepdims=True)
    return values * lax.rsqrt(mean_sq + eps)


def attend_kernel(qd_ref, kd_ref, q_ref, pk_ref, k_ref, pv_ref, v_ref, o_ref, bias):
    rows = q_ref.shape[0]
    span = WIN + QB

    @pl.when(pl.program_id(0) == 0)
    def _():
        for i in range(rows // QB):
            far = lax.broadcasted_iota(jnp.int32, (QB, span), 0) - (
                lax.broadcasted_iota(jnp.int32, (QB, span), 1) - WIN
            )
            same = qd_ref[i * QB : (i + 1) * QB, :] == kd_ref[:, i * QB : i * QB + span]
            allowed = (far >= 0) & (far < WIN) & same
            bias[i] = jnp.where(allowed, 0.0, -1e30).astype(f32)

    scale = 1.0 / HD**0.5
    nt = (((1,), (1,)), ((), ()))
    for i in range(rows // QB):
        first = i * QB
        cut = WIN - first
        q = q_ref[first : first + QB, :]
        own = first + QB
        s_a = lax.dot_general(q, pk_ref[first:, :], nt, preferred_element_type=f32)
        s_b = lax.dot_general(q, k_ref[:own, :], nt, preferred_element_type=f32)
        s_a = s_a * scale + bias[i, :, :cut]
        s_b = s_b * scale + bias[i, :, cut:]
        top = jnp.maximum(
            jnp.max(s_a, axis=-1, keepdims=True), jnp.max(s_b, axis=-1, keepdims=True)
        )
        e_a = jnp.exp(s_a - top)
        e_b = jnp.exp(s_b - top)
        inv = 1.0 / (
            jnp.sum(e_a, axis=-1, keepdims=True) + jnp.sum(e_b, axis=-1, keepdims=True)
        )
        mixed = jnp.dot((e_a * inv).astype(bf16), pv_ref[first:, :], preferred_element_type=f32)
        mixed += jnp.dot((e_b * inv).astype(bf16), v_ref[:own, :], preferred_element_type=f32)
        o_ref[first : first + QB, :] = mixed.astype(bf16)


def attend(q_docs, k_docs, q, pk, k, pv, v):
    rows, width = q.shape
    col = pl.BlockSpec((rows, HD), lambda h: (0, h))
    return pl.pallas_call(
        attend_kernel,
        grid=(width // HD,),
        in_specs=[
            pl.BlockSpec((rows, 1), lambda h: (0, 0)),
            pl.BlockSpec((1, rows + WIN), lambda h: (0, 0)),
            col, col, col, col, col,
        ],
        out_specs=col,
        out_shape=jax.ShapeDtypeStruct((rows, width), bf16),
        scratch_shapes=[pltpu.VMEM((rows // QB, QB, WIN + QB), f32)],
        compiler_params=params(),
        cost_estimate=cost(16e9, 6 * MIB),
    )(q_docs, k_docs, q, pk, k, pv, v)


def pool_kernel(mine, other, w_mine, w_other, bytes_ref, ids, enc, sums, lead):
    half = bytes_ref.shape[0] // 2
    for i in range(2):
        part = slice(i * half, (i + 1) * half)
        term = jnp.dot(mine[part, :], w_mine[...], preferred_element_type=f32)
        term += jnp.dot(other[part, :], w_other[...], preferred_element_type=f32)
        enc[part, :] = (bytes_ref[part, :].astype(f32) + term).astype(bf16)
    rows = bytes_ref.shape[0]
    slot = lax.broadcasted_iota(jnp.int32, (CAP, rows), 0)
    member = (ids[...] == slot).astype(f32).astype(bf16)
    sums[...] = jnp.dot(member, enc[...], preferred_element_type=f32)
    leading = jnp.broadcast_to((ids[...] < 0).astype(f32), (8, rows))
    count = jnp.sum(leading, axis=1, keepdims=True)
    total = jnp.dot(leading.astype(bf16), enc[...], preferred_element_type=f32)
    at = lax.broadcasted_iota(jnp.int32, total.shape, 0)
    lead[...] = jnp.where(at == 1, count, total)


def pool(mine, other, w_mine, w_other, byte_states, ids_row):
    rows, width = byte_states.shape
    return pl.pallas_call(
        pool_kernel,
        in_specs=[VM] * 6,
        out_specs=[VM] * 3,
        out_shape=[
            jax.ShapeDtypeStruct((rows, width), bf16),
            jax.ShapeDtypeStruct((CAP, width), f32),
            jax.ShapeDtypeStruct((8, width), f32),
        ],
        compiler_params=params(),
        cost_estimate=cost(4e9, 10 * MIB),
    )(mine, other, w_mine, w_other, byte_states, ids_row)


def main_kernel(pieces, n_operands, gn, *refs):
    operands = refs[:n_operands]
    keep, send, wg, wu, wd, hid, sems = refs[n_operands:]
    s = lax.axis_index("seq")
    h = lax.axis_index("head")
    copies = {"g": [], "u": [], "d": []}
    for kind, number, prefix, ways in pieces:
        ref = operands[number]
        depth = ref.shape[-1] if kind == "d" else ref.shape[-2] // len(ways)
        for m, way in enumerate(ways):
            index = s
            for bit in way:
                index = flip(index, bit)
            place = pl.multiple_of(index * depth, depth) if depth < wg.shape[0] else 0
            if kind == "d":
                source = ref.at[m]
                target = wd.at[:, pl.ds(place, depth)]
            else:
                source = ref.at[prefix + (pl.ds(m * depth, depth),)]
                target = (wg if kind == "g" else wu).at[pl.ds(place, depth)]
            at = sum(len(group) for group in copies.values())
            copies[kind].append(pltpu.make_async_copy(source, target, sems.at[at]))
    for kind in "gud":
        for copy in copies[kind]:
            copy.start()
    for copy in copies["g"] + copies["u"]:
        copy.wait()
    units = wg.shape[1]
    tile = 384
    for t in range(units // tile):
        cols = slice(t * tile, (t + 1) * tile)
        gate = jnp.dot(gn[...], wg[:, cols], preferred_element_type=f32)
        up = jnp.dot(gn[...], wu[:, cols], preferred_element_type=f32)
        hid[:, cols] = (jax.nn.silu(gate) * up).astype(bf16)
    for copy in copies["d"]:
        copy.wait()
    width = send.shape[1]
    step = 512
    for t in range(width // step):
        out = pl.ds(t * step, step)
        there = pl.ds(pl.multiple_of((1 - h) * width + t * step, step), step)
        send[:, out] = jnp.dot(hid[...], wd[:, there], preferred_element_type=f32).astype(bf16)
    for t in range(width // step):
        out = pl.ds(t * step, step)
        here = pl.ds(pl.multiple_of(h * width + t * step, step), step)
        keep[:, out] = jnp.dot(hid[...], wd[:, here], preferred_element_type=f32)


def main_layer(gn, operands, pieces):
    tokens, dm = gn.shape
    units = operands[0].shape[-1]
    n_copies = sum(len(ways) for _, _, _, ways in pieces)
    return pl.pallas_call(
        functools.partial(main_kernel, pieces, len(operands)),
        in_specs=[VM] + [ANY] * len(operands),
        out_specs=[VM, VM],
        out_shape=[
            jax.ShapeDtypeStruct((tokens, dm // 2), f32),
            jax.ShapeDtypeStruct((tokens, dm // 2), bf16),
        ],
        scratch_shapes=[
            pltpu.VMEM((dm, units), bf16),
            pltpu.VMEM((dm, units), bf16),
            pltpu.VMEM((units, dm), bf16),
            pltpu.VMEM((tokens, units), bf16),
            pltpu.SemaphoreType.DMA((n_copies,)),
        ],
        compiler_params=params(),
        cost_estimate=cost(8e9, 20 * MIB),
    )(gn, *operands)


def back_kernel(starts, mine, other, w_back, back, tail):
    h = lax.axis_index("head")
    half = mine.shape[1]
    w_mine = w_back[pl.ds(pl.multiple_of(h * half, half), half), :]
    w_other = w_back[pl.ds(pl.multiple_of((1 - h) * half, half), half), :]
    total = jnp.dot(mine[...], w_mine, preferred_element_type=f32)
    total += jnp.dot(other[...], w_other, preferred_element_type=f32)
    back[...] = total.astype(bf16)
    row = lax.broadcasted_iota(jnp.int32, (16, CAP), 0)
    slot = lax.broadcasted_iota(jnp.int32, (16, CAP), 1)
    pick = (slot == starts[0] - 2 + row) & (row < 2)
    tail[...] = jnp.dot(
        pick.astype(f32).astype(bf16), back[...], preferred_element_type=f32
    ).astype(bf16)


def back_rows(starts, mine, other, w_back):
    width = w_back.shape[1]
    return pl.pallas_call(
        back_kernel,
        in_specs=[pl.BlockSpec(memory_space=pltpu.SMEM), VM, VM, VM],
        out_specs=[VM, VM],
        out_shape=[
            jax.ShapeDtypeStruct((mine.shape[0], width), bf16),
            jax.ShapeDtypeStruct((16, width), bf16),
        ],
        compiler_params=params(),
        cost_estimate=cost(3e9, 8 * MIB),
    )(starts, mine, other, w_back)


def lift_kernel(ids, enc, back, tail, out):
    group = ids[...]
    rows = group.shape[0]
    slot = lax.broadcasted_iota(jnp.int32, (rows, CAP), 1)
    pick = (group - 1 == slot).astype(f32).astype(bf16)
    lifted = jnp.dot(pick, back[...], preferred_element_type=f32)
    lifted += jnp.where(group == -1, tail[0:1, :].astype(f32), 0.0)
    lifted += jnp.where(group == 0, tail[1:2, :].astype(f32), 0.0)
    out[...] = (enc[...].astype(f32) + lifted).astype(bf16)


def lift(ids_col, encoded, back, tail):
    rows, width = encoded.shape
    block = 256
    return pl.pallas_call(
        lift_kernel,
        grid=(rows // block,),
        in_specs=[
            pl.BlockSpec((block, 1), lambda i: (i, 0)),
            pl.BlockSpec((block, width), lambda i: (i, 0)),
            pl.BlockSpec(back.shape, lambda i: (0, 0)),
            pl.BlockSpec(tail.shape, lambda i: (0, 0)),
        ],
        out_specs=pl.BlockSpec((block, width), lambda i: (i, 0)),
        out_shape=jax.ShapeDtypeStruct((rows, width), bf16),
        compiler_params=params(),
        cost_estimate=cost(2e9, 6 * MIB),
    )(ids_col, encoded, back, tail)


def gather_weights(w_gate, w_up, w_down, role):
    n_seq = lax.axis_size("seq")
    units = w_gate.shape[1] // 2

    if n_seq != 16:
        mine = role * units
        gate = lax.dynamic_slice_in_dim(lax.all_gather(w_gate, "seq", axis=0, tiled=True), mine, units, 1)
        up = lax.dynamic_slice_in_dim(lax.all_gather(w_up, "seq", axis=0, tiled=True), mine, units, 1)
        down = lax.dynamic_slice_in_dim(lax.all_gather(w_down, "seq", axis=1, tiled=True), mine, units, 0)
        whole = ((),)
        pieces = [("g", 0, (), whole), ("u", 1, (), whole), ("d", 2, (), whole)]
        return [gate, up, down[None]], pieces

    def half(of):
        return (
            jnp.stack([
                lax.dynamic_slice_in_dim(w_gate, of * units, units, 1),
                lax.dynamic_slice_in_dim(w_up, of * units, units, 1),
            ]),
            lax.dynamic_slice_in_dim(w_down, of * units, units, 0),
        )

    gu_mine, dn_mine = half(role)
    gu_theirs, dn_theirs = half(1 - role)
    operands, pieces = [], []

    def add_gu(block, ways):
        pieces.append(("g", len(operands), (0,), ways))
        pieces.append(("u", len(operands), (1,), ways))
        operands.append(block)

    def add_one(kind, block, ways):
        pieces.append((kind, len(operands), (), ways))
        operands.append(block)

    def along(ways, *bits):
        return tuple(way + bits for way in ways)

    def spread_gu(block, ways):
        by_x, by_y = swapped(block, 1), swapped(block, 2)
        gate_xy, up_xy = swapped(by_x[0], 2), swapped(by_y[1], 1)
        add_gu(block, ways)
        add_gu(by_x, along(ways, 1))
        add_gu(by_y, along(ways, 2))
        add_one("g", gate_xy, along(ways, 1, 2))
        add_one("u", up_xy, along(ways, 1, 2))

    def spread_dn(block, ways, first):
        by_x, by_y = swapped(block, 1), swapped(block, 2)
        by_xy = swapped(by_x, 2) if first == 1 else swapped(by_y, 1)
        add_one("d", block, ways)
        add_one("d", by_x, along(ways, 1))
        add_one("d", by_y, along(ways, 2))
        add_one("d", by_xy, along(ways, 1, 2))

    here, beside = ((),), ((PAIR,),)
    across = ((8,), (8, PAIR))
    gu_beside = swapped(gu_theirs, PAIR)
    gu_across = [swapped(gu_mine, 8), swapped(gu_theirs, 8 ^ PAIR)]
    dn_beside = swapped(dn_theirs, PAIR)
    dn_across = [swapped(dn_mine, 8), swapped(dn_theirs, 8 ^ PAIR)]
    spread_gu(gu_mine, here)
    spread_gu(gu_beside, beside)
    spread_gu(jnp.concatenate(gu_across, axis=1), across)
    spread_dn(jnp.stack([dn_mine, dn_beside]), here + beside, 1)
    spread_dn(jnp.stack(dn_across), across, 2)
    return operands, pieces


def by_head(mine, other, head, axis):
    low = jnp.where(head == 0, mine, other)
    high = jnp.where(head == 0, other, mine)
    return jnp.concatenate([low, high], axis=axis)


def body(byte_states, doc_ids, boundary_flags, w_qkv, w_out, w_span, w_gate, w_up, w_down, w_back):
    rows, width = byte_states.shape
    s = lax.axis_index("seq")
    head = lax.axis_index("head")
    role = (s // PAIR) % 2

    half = lax.dynamic_slice_in_dim(byte_states, head * (rows // 2), rows // 2, 0)
    prior_half = shifted(half, "seq", 1)
    prior_docs = jnp.where(s == 0, -1, shifted(doc_ids, "seq", 1))
    w_out_other = swapped(w_out, 1, "head")
    operands, pieces = gather_weights(w_gate, w_up, w_down, role)

    normed = rms_rows(byte_states.astype(f32)).astype(bf16)
    queries = jnp.dot(normed, w_qkv[0], preferred_element_type=f32).astype(bf16)
    keys = jnp.dot(normed, w_qkv[1], preferred_element_type=f32).astype(bf16)
    values = jnp.dot(normed, w_qkv[2], preferred_element_type=f32).astype(bf16)
    prior = by_head(prior_half, swapped(prior_half, 1, "head"), head, 0)
    prior_normed = rms_rows(prior.astype(f32)).astype(bf16)
    prior_keys = jnp.dot(prior_normed, w_qkv[1], preferred_element_type=f32).astype(bf16)
    prior_values = jnp.dot(prior_normed, w_qkv[2], preferred_element_type=f32).astype(bf16)

    all_docs = jnp.concatenate([prior_docs, doc_ids])
    attended = attend(
        doc_ids[:, None], all_docs[None, :], queries, prior_keys, keys, prior_values, values
    )
    attended_other = swapped(attended, 1, "head")

    local_ids = jnp.cumsum(boundary_flags, dtype=jnp.int32) - 1
    starts = jnp.sum(boundary_flags, dtype=jnp.int32)
    encoded, sums, lead = pool(
        attended, attended_other, w_out, w_out_other, byte_states, local_ids[None, :]
    )
    following = shifted(lead, "seq", -1)
    slots = jnp.arange(CAP, dtype=jnp.int32)
    counts = jnp.sum(local_ids[None, :] == slots[:, None], axis=1).astype(f32)
    last_slot = slots == starts - 1
    sums = sums + jnp.where(last_slot[:, None], following[0:1], f32(0.0))
    counts = counts + jnp.where(last_slot, following[1, 0], f32(0.0))
    pooled = (sums / jnp.maximum(counts, 1.0)[:, None]).astype(bf16)

    share = lax.dynamic_slice_in_dim(pooled, head * (width // 2), width // 2, 1)
    got = swapped(share, PAIR)
    pooled_partner = by_head(got, swapped(got, 1, "head"), head, 1)

    def enter(values):
        group_in = jnp.dot(values, w_span, preferred_element_type=f32).astype(bf16)
        return group_in, rms_rows(group_in.astype(f32)).astype(bf16)

    group_in, group_normed = enter(pooled)
    _, partner_normed = enter(pooled_partner)
    keep_p, send_p = main_layer(partner_normed, operands, pieces)
    partner_sum = (keep_p + swapped(send_p, 1, "head").astype(f32)).astype(bf16)
    group_normed, partner_sum = lax.optimization_barrier((group_normed, partner_sum))
    from_partner = swapped(partner_sum, PAIR)
    keep, send = main_layer(group_normed, operands, pieces)
    own_sum = keep + swapped(send, 1, "head").astype(f32)
    dm_half = keep.shape[1]
    in_half = lax.dynamic_slice_in_dim(group_in, head * dm_half, dm_half, 1)
    main = (in_half.astype(f32) + own_sum + from_partner.astype(f32)).astype(bf16)
    main_other = swapped(main, 1, "head")
    back, tail = back_rows(starts[None], main, main_other, w_back)
    prior_tail = shifted(tail, "seq", 1)
    return lift(local_ids[:, None], encoded, back, prior_tail)


def solution(mesh):
    placed = (
        P("seq", None),
        P("seq"),
        P("seq"),
        P(None, None, "head"),
        P("head", None),
        P(),
        P("seq", "head"),
        P("seq", "head"),
        P("head", "seq"),
        P(),
    )
    return jax.shard_map(
        body, mesh=mesh, in_specs=placed, out_specs=P("seq", None), check_vma=False
    )
```

```python
import functools

import jax
import jax.numpy as jnp
from jax import lax
from jax.experimental import pallas as pl
from jax.experimental.pallas import tpu as pltpu
from jax.sharding import PartitionSpec as P

HD = 128
WIN = 1024
CAP = 512
QB = 256
PAIR = 4

eps = 1e-06
f32 = jnp.float32
bf16 = jnp.bfloat16
VM = pl.BlockSpec(memory_space=pltpu.VMEM)
ANY = pl.BlockSpec(memory_space=pl.ANY)
MIB = 1 << 20


def shifted(block, axis, distance):
    devices = range(lax.axis_size(axis))
    route = [(i - distance, i) for i in devices if i - distance in devices]
    return lax.ppermute(block, axis, route)


def swapped(block, bit, axis="seq"):
    return lax.ppermute(block, axis, [(i, i ^ bit) for i in range(lax.axis_size(axis))])


def flip(number, bit):
    return number + bit - 2 * bit * ((number // bit) % 2)


def params(mib=48):
    return pltpu.CompilerParams(vmem_limit_bytes=mib * MIB)


def cost(flops, moved):
    return pl.CostEstimate(flops=int(flops), bytes_accessed=int(moved), transcendentals=0)


def rms_rows(values):
    mean_sq = jnp.mean(values * values, axis=-1, keepdims=True)
    return values * lax.rsqrt(mean_sq + eps)


def attend_kernel(qd_ref, kd_ref, q_ref, pk_ref, k_ref, pv_ref, v_ref, o_ref, bias):
    rows = q_ref.shape[0]
    span = WIN + QB

    @pl.when(pl.program_id(0) == 0)
    def _():
        for i in range(rows // QB):
            far = lax.broadcasted_iota(jnp.int32, (QB, span), 0) - (
                lax.broadcasted_iota(jnp.int32, (QB, span), 1) - WIN
            )
            same = qd_ref[i * QB : (i + 1) * QB, :] == kd_ref[:, i * QB : i * QB + span]
            allowed = (far >= 0) & (far < WIN) & same
            bias[i] = jnp.where(allowed, 0.0, -1e30).astype(f32)

    scale = 1.0 / HD**0.5
    nt = (((1,), (1,)), ((), ()))
    for i in range(rows // QB):
        first = i * QB
        cut = WIN - first
        q = q_ref[first : first + QB, :]
        own = first + QB
        s_a = lax.dot_general(q, pk_ref[first:, :], nt, preferred_element_type=f32)
        s_b = lax.dot_general(q, k_ref[:own, :], nt, preferred_element_type=f32)
        s_a = s_a * scale + bias[i, :, :cut]
        s_b = s_b * scale + bias[i, :, cut:]
        top = jnp.maximum(
            jnp.max(s_a, axis=-1, keepdims=True), jnp.max(s_b, axis=-1, keepdims=True)
        )
        e_a = jnp.exp(s_a - top)
        e_b = jnp.exp(s_b - top)
        inv = 1.0 / (
            jnp.sum(e_a, axis=-1, keepdims=True) + jnp.sum(e_b, axis=-1, keepdims=True)
        )
        mixed = jnp.dot((e_a * inv).astype(bf16), pv_ref[first:, :], preferred_element_type=f32)
        mixed += jnp.dot((e_b * inv).astype(bf16), v_ref[:own, :], preferred_element_type=f32)
        o_ref[first : first + QB, :] = mixed.astype(bf16)


def attend(q_docs, k_docs, q, pk, k, pv, v):
    rows, width = q.shape
    col = pl.BlockSpec((rows, HD), lambda h: (0, h))
    return pl.pallas_call(
        attend_kernel,
        grid=(width // HD,),
        in_specs=[
            pl.BlockSpec((rows, 1), lambda h: (0, 0)),
            pl.BlockSpec((1, rows + WIN), lambda h: (0, 0)),
            col, col, col, col, col,
        ],
        out_specs=col,
        out_shape=jax.ShapeDtypeStruct((rows, width), bf16),
        scratch_shapes=[pltpu.VMEM((rows // QB, QB, WIN + QB), f32)],
        compiler_params=params(),
        cost_estimate=cost(16e9, 6 * MIB),
    )(q_docs, k_docs, q, pk, k, pv, v)


def pool_kernel(mine, other, w_mine, w_other, bytes_ref, ids, enc, sums, lead):
    half = bytes_ref.shape[0] // 2
    for i in range(2):
        part = slice(i * half, (i + 1) * half)
        term = jnp.dot(mine[part, :], w_mine[...], preferred_element_type=f32)
        term += jnp.dot(other[part, :], w_other[...], preferred_element_type=f32)
        enc[part, :] = (bytes_ref[part, :].astype(f32) + term).astype(bf16)
    rows = bytes_ref.shape[0]
    slot = lax.broadcasted_iota(jnp.int32, (CAP, rows), 0)
    member = (ids[...] == slot).astype(f32).astype(bf16)
    sums[...] = jnp.dot(member, enc[...], preferred_element_type=f32)
    leading = jnp.broadcast_to((ids[...] < 0).astype(f32), (8, rows))
    count = jnp.sum(leading, axis=1, keepdims=True)
    total = jnp.dot(leading.astype(bf16), enc[...], preferred_element_type=f32)
    at = lax.broadcasted_iota(jnp.int32, total.shape, 0)
    lead[...] = jnp.where(at == 1, count, total)


def pool(mine, other, w_mine, w_other, byte_states, ids_row):
    rows, width = byte_states.shape
    return pl.pallas_call(
        pool_kernel,
        in_specs=[VM] * 6,
        out_specs=[VM] * 3,
        out_shape=[
            jax.ShapeDtypeStruct((rows, width), bf16),
            jax.ShapeDtypeStruct((CAP, width), f32),
            jax.ShapeDtypeStruct((8, width), f32),
        ],
        compiler_params=params(),
        cost_estimate=cost(4e9, 10 * MIB),
    )(mine, other, w_mine, w_other, byte_states, ids_row)


def main_kernel(n_pairs, sources, gn, *refs):
    gus, dns = refs[:n_pairs], refs[n_pairs : 2 * n_pairs]
    keep, send, wg, wu, wd, hid, sem_g, sem_u, sem_d = refs[2 * n_pairs :]
    depth = wg.shape[0] // (2 * n_pairs)
    s = lax.axis_index("seq")
    h = lax.axis_index("head")
    copies_g, copies_u, copies_d = [], [], []
    for j in range(n_pairs):
        for m in range(2):
            if sources is None:
                place = (2 * j + m) * depth
            else:
                index = s
                for bit in sources[j][m]:
                    index = flip(index, bit)
                place = pl.multiple_of(index * depth, depth)
            rows = pl.ds(m * depth, depth)
            at = 2 * j + m
            copies_g.append(pltpu.make_async_copy(
                gus[j].at[0, rows], wg.at[pl.ds(place, depth)], sem_g.at[at]))
            copies_u.append(pltpu.make_async_copy(
                gus[j].at[1, rows], wu.at[pl.ds(place, depth)], sem_u.at[at]))
            copies_d.append(pltpu.make_async_copy(
                dns[j].at[m], wd.at[:, pl.ds(place, depth)], sem_d.at[at]))
    for copy in copies_g + copies_u + copies_d:
        copy.start()
    for copy in copies_g + copies_u:
        copy.wait()
    units = wg.shape[1]
    tile = 384
    for t in range(units // tile):
        cols = slice(t * tile, (t + 1) * tile)
        gate = jnp.dot(gn[...], wg[:, cols], preferred_element_type=f32)
        up = jnp.dot(gn[...], wu[:, cols], preferred_element_type=f32)
        hid[:, cols] = (jax.nn.silu(gate) * up).astype(bf16)
    for copy in copies_d:
        copy.wait()
    width = send.shape[1]
    step = 512
    for t in range(width // step):
        out = pl.ds(t * step, step)
        there = pl.ds(pl.multiple_of((1 - h) * width + t * step, step), step)
        send[:, out] = jnp.dot(hid[...], wd[:, there], preferred_element_type=f32).astype(bf16)
    for t in range(width // step):
        out = pl.ds(t * step, step)
        here = pl.ds(pl.multiple_of(h * width + t * step, step), step)
        keep[:, out] = jnp.dot(hid[...], wd[:, here], preferred_element_type=f32)


def main_layer(gn, gus, dns, sources):
    tokens, dm = gn.shape
    units = gus[0].shape[2]
    n_pairs = len(gus)
    n_blocks = 2 * n_pairs
    return pl.pallas_call(
        functools.partial(main_kernel, n_pairs, sources),
        in_specs=[VM] + [ANY] * (2 * n_pairs),
        out_specs=[VM, VM],
        out_shape=[
            jax.ShapeDtypeStruct((tokens, dm // 2), f32),
            jax.ShapeDtypeStruct((tokens, dm // 2), bf16),
        ],
        scratch_shapes=[
            pltpu.VMEM((dm, units), bf16),
            pltpu.VMEM((dm, units), bf16),
            pltpu.VMEM((units, dm), bf16),
            pltpu.VMEM((tokens, units), bf16),
            pltpu.SemaphoreType.DMA((n_blocks,)),
            pltpu.SemaphoreType.DMA((n_blocks,)),
            pltpu.SemaphoreType.DMA((n_blocks,)),
        ],
        compiler_params=params(),
        cost_estimate=cost(8e9, 20 * MIB),
    )(gn, *gus, *dns)


def back_kernel(starts, mine, other, w_back, back, tail):
    h = lax.axis_index("head")
    half = mine.shape[1]
    w_mine = w_back[pl.ds(pl.multiple_of(h * half, half), half), :]
    w_other = w_back[pl.ds(pl.multiple_of((1 - h) * half, half), half), :]
    total = jnp.dot(mine[...], w_mine, preferred_element_type=f32)
    total += jnp.dot(other[...], w_other, preferred_element_type=f32)
    back[...] = total.astype(bf16)
    row = lax.broadcasted_iota(jnp.int32, (16, CAP), 0)
    slot = lax.broadcasted_iota(jnp.int32, (16, CAP), 1)
    pick = (slot == starts[0] - 2 + row) & (row < 2)
    tail[...] = jnp.dot(
        pick.astype(f32).astype(bf16), back[...], preferred_element_type=f32
    ).astype(bf16)


def back_rows(starts, mine, other, w_back):
    width = w_back.shape[1]
    return pl.pallas_call(
        back_kernel,
        in_specs=[pl.BlockSpec(memory_space=pltpu.SMEM), VM, VM, VM],
        out_specs=[VM, VM],
        out_shape=[
            jax.ShapeDtypeStruct((mine.shape[0], width), bf16),
            jax.ShapeDtypeStruct((16, width), bf16),
        ],
        compiler_params=params(),
        cost_estimate=cost(3e9, 8 * MIB),
    )(starts, mine, other, w_back)


def lift_kernel(ids, enc, back, tail, out):
    group = ids[...]
    rows = group.shape[0]
    slot = lax.broadcasted_iota(jnp.int32, (rows, CAP), 1)
    pick = (group - 1 == slot).astype(f32).astype(bf16)
    lifted = jnp.dot(pick, back[...], preferred_element_type=f32)
    lifted += jnp.where(group == -1, tail[0:1, :].astype(f32), 0.0)
    lifted += jnp.where(group == 0, tail[1:2, :].astype(f32), 0.0)
    out[...] = (enc[...].astype(f32) + lifted).astype(bf16)


def lift(ids_col, encoded, back, tail):
    rows, width = encoded.shape
    block = 256
    return pl.pallas_call(
        lift_kernel,
        grid=(rows // block,),
        in_specs=[
            pl.BlockSpec((block, 1), lambda i: (i, 0)),
            pl.BlockSpec((block, width), lambda i: (i, 0)),
            pl.BlockSpec(back.shape, lambda i: (0, 0)),
            pl.BlockSpec(tail.shape, lambda i: (0, 0)),
        ],
        out_specs=pl.BlockSpec((block, width), lambda i: (i, 0)),
        out_shape=jax.ShapeDtypeStruct((rows, width), bf16),
        compiler_params=params(),
        cost_estimate=cost(2e9, 6 * MIB),
    )(ids_col, encoded, back, tail)


def gather_weights(w_gate, w_up, w_down, role):
    n_seq = lax.axis_size("seq")
    units = w_gate.shape[1] // 2
    depth = w_gate.shape[0]

    if n_seq != 16:
        mine = role * units
        gate = lax.dynamic_slice_in_dim(lax.all_gather(w_gate, "seq", axis=0, tiled=True), mine, units, 1)
        up = lax.dynamic_slice_in_dim(lax.all_gather(w_up, "seq", axis=0, tiled=True), mine, units, 1)
        down = lax.dynamic_slice_in_dim(lax.all_gather(w_down, "seq", axis=1, tiled=True), mine, units, 0)
        both = jnp.stack([gate, up])
        gus = [both[:, i : i + 256] for i in range(0, both.shape[1], 256)]
        dns = [
            jnp.stack([down[:, i : i + 128], down[:, i + 128 : i + 256]])
            for i in range(0, down.shape[1], 256)
        ]
        return gus, dns, None

    def half(of):
        return (
            jnp.stack([
                lax.dynamic_slice_in_dim(w_gate, of * units, units, 1),
                lax.dynamic_slice_in_dim(w_up, of * units, units, 1),
            ]),
            lax.dynamic_slice_in_dim(w_down, of * units, units, 0),
        )

    gu_mine, dn_mine = half(role)
    gu_theirs, dn_theirs = half(1 - role)
    gu = jnp.concatenate([gu_mine, swapped(gu_theirs, PAIR)], axis=1)
    gu, dn_theirs = lax.optimization_barrier((gu, dn_theirs))
    dn = jnp.stack([dn_mine, swapped(dn_theirs, PAIR)])

    gu_z = swapped(gu, 8)
    gu_x, gu_y = swapped(gu, 1), swapped(gu, 2)
    dn_z = swapped(dn, 8)
    gu_xy = jnp.stack([swapped(gu_x[0], 2), swapped(gu_y[1], 1)])
    gu_zx, gu_zy = swapped(gu_z, 1), swapped(gu_z, 2)
    dn_x, dn_y = swapped(dn, 1), swapped(dn, 2)
    gu_zxy = jnp.stack([swapped(gu_zx[0], 2), swapped(gu_zy[1], 1)])
    dn_xy = swapped(dn_x, 2)
    dn_zx, dn_zy = swapped(dn_z, 1), swapped(dn_z, 2)
    dn_zxy = swapped(dn_zy, 1)
    gus = [gu, gu_z, gu_x, gu_y, gu_xy, gu_zx, gu_zy, gu_zxy]
    dns = [dn, dn_z, dn_x, dn_y, dn_xy, dn_zx, dn_zy, dn_zxy]
    ways = [(), (8,), (1,), (2,), (1, 2), (8, 1), (8, 2), (8, 1, 2)]
    sources = [(way, way + (PAIR,)) for way in ways]
    return gus, dns, sources


def by_head(mine, other, head, axis):
    low = jnp.where(head == 0, mine, other)
    high = jnp.where(head == 0, other, mine)
    return jnp.concatenate([low, high], axis=axis)


def body(byte_states, doc_ids, boundary_flags, w_qkv, w_out, w_span, w_gate, w_up, w_down, w_back):
    rows, width = byte_states.shape
    s = lax.axis_index("seq")
    head = lax.axis_index("head")
    role = (s // PAIR) % 2

    half = lax.dynamic_slice_in_dim(byte_states, head * (rows // 2), rows // 2, 0)
    prior_half = shifted(half, "seq", 1)
    prior_docs = jnp.where(s == 0, -1, shifted(doc_ids, "seq", 1))
    w_out_other = swapped(w_out, 1, "head")
    gus, dns, sources = gather_weights(w_gate, w_up, w_down, role)

    normed = rms_rows(byte_states.astype(f32)).astype(bf16)
    queries = jnp.dot(normed, w_qkv[0], preferred_element_type=f32).astype(bf16)
    keys = jnp.dot(normed, w_qkv[1], preferred_element_type=f32).astype(bf16)
    values = jnp.dot(normed, w_qkv[2], preferred_element_type=f32).astype(bf16)
    prior = by_head(prior_half, swapped(prior_half, 1, "head"), head, 0)
    prior_normed = rms_rows(prior.astype(f32)).astype(bf16)
    prior_keys = jnp.dot(prior_normed, w_qkv[1], preferred_element_type=f32).astype(bf16)
    prior_values = jnp.dot(prior_normed, w_qkv[2], preferred_element_type=f32).astype(bf16)

    all_docs = jnp.concatenate([prior_docs, doc_ids])
    attended = attend(
        doc_ids[:, None], all_docs[None, :], queries, prior_keys, keys, prior_values, values
    )
    attended_other = swapped(attended, 1, "head")

    local_ids = jnp.cumsum(boundary_flags, dtype=jnp.int32) - 1
    starts = jnp.sum(boundary_flags, dtype=jnp.int32)
    encoded, sums, lead = pool(
        attended, attended_other, w_out, w_out_other, byte_states, local_ids[None, :]
    )
    following = shifted(lead, "seq", -1)
    slots = jnp.arange(CAP, dtype=jnp.int32)
    counts = jnp.sum(local_ids[None, :] == slots[:, None], axis=1).astype(f32)
    last_slot = slots == starts - 1
    sums = sums + jnp.where(last_slot[:, None], following[0:1], f32(0.0))
    counts = counts + jnp.where(last_slot, following[1, 0], f32(0.0))
    pooled = (sums / jnp.maximum(counts, 1.0)[:, None]).astype(bf16)

    share = lax.dynamic_slice_in_dim(pooled, head * (width // 2), width // 2, 1)
    got = swapped(share, PAIR)
    pooled_partner = by_head(got, swapped(got, 1, "head"), head, 1)

    def enter(values):
        group_in = jnp.dot(values, w_span, preferred_element_type=f32).astype(bf16)
        return group_in, rms_rows(group_in.astype(f32)).astype(bf16)

    group_in, group_normed = enter(pooled)
    _, partner_normed = enter(pooled_partner)
    keep_p, send_p = main_layer(partner_normed, gus, dns, sources)
    partner_sum = (keep_p + swapped(send_p, 1, "head").astype(f32)).astype(bf16)
    from_partner = swapped(partner_sum, PAIR)
    group_normed, partner_sum = lax.optimization_barrier((group_normed, partner_sum))
    keep, send = main_layer(group_normed, gus, dns, sources)
    piece = send.shape[0] // 2
    arrived = [
        swapped(send[i * piece : (i + 1) * piece], 1, "head").astype(f32) for i in range(2)
    ]
    own_sum = keep + jnp.concatenate(arrived)
    own_sum, from_partner = lax.optimization_barrier((own_sum, from_partner))
    dm_half = keep.shape[1]
    in_half = lax.dynamic_slice_in_dim(group_in, head * dm_half, dm_half, 1)
    main = (in_half.astype(f32) + own_sum + from_partner.astype(f32)).astype(bf16)
    main_other = swapped(main, 1, "head")
    back, tail = back_rows(starts[None], main, main_other, w_back)
    prior_tail = shifted(tail, "seq", 1)
    return lift(local_ids[:, None], encoded, back, prior_tail)


def solution(mesh):
    placed = (
        P("seq", None),
        P("seq"),
        P("seq"),
        P(None, None, "head"),
        P("head", None),
        P(),
        P("seq", "head"),
        P("seq", "head"),
        P("head", "seq"),
        P(),
    )
    return jax.shard_map(
        body, mesh=mesh, in_specs=placed, out_specs=P("seq", None), check_vma=False
    )
```

```python
import functools

import jax
import jax.numpy as jnp
from jax import lax
from jax.experimental import pallas as pl
from jax.experimental.pallas import tpu as pltpu
from jax.sharding import PartitionSpec as P

HD = 128
WIN = 1024
CAP = 512
QB = 256
PAIR = 4

eps = 1e-06
f32 = jnp.float32
bf16 = jnp.bfloat16
VM = pl.BlockSpec(memory_space=pltpu.VMEM)
ANY = pl.BlockSpec(memory_space=pl.ANY)
MIB = 1 << 20


def shifted(block, axis, distance):
    devices = range(lax.axis_size(axis))
    route = [(i - distance, i) for i in devices if i - distance in devices]
    return lax.ppermute(block, axis, route)


def swapped(block, bit, axis="seq"):
    return lax.ppermute(block, axis, [(i, i ^ bit) for i in range(lax.axis_size(axis))])


def flip(number, bit):
    return number + bit - 2 * bit * ((number // bit) % 2)


def params(mib=48):
    return pltpu.CompilerParams(vmem_limit_bytes=mib * MIB)


def cost(flops, moved):
    return pl.CostEstimate(flops=int(flops), bytes_accessed=int(moved), transcendentals=0)


def rms_rows(values):
    mean_sq = jnp.mean(values * values, axis=-1, keepdims=True)
    return values * lax.rsqrt(mean_sq + eps)


def attend_kernel(qd_ref, kd_ref, q_ref, pk_ref, k_ref, pv_ref, v_ref, o_ref, bias):
    rows = q_ref.shape[0]
    span = WIN + QB

    @pl.when(pl.program_id(0) == 0)
    def _():
        for i in range(rows // QB):
            far = lax.broadcasted_iota(jnp.int32, (QB, span), 0) - (
                lax.broadcasted_iota(jnp.int32, (QB, span), 1) - WIN
            )
            same = qd_ref[i * QB : (i + 1) * QB, :] == kd_ref[:, i * QB : i * QB + span]
            allowed = (far >= 0) & (far < WIN) & same
            bias[i] = jnp.where(allowed, 0.0, -1e30).astype(f32)

    scale = 1.0 / HD**0.5
    nt = (((1,), (1,)), ((), ()))
    for i in range(rows // QB):
        first = i * QB
        cut = WIN - first
        q = q_ref[first : first + QB, :]
        own = first + QB
        s_a = lax.dot_general(q, pk_ref[first:, :], nt, preferred_element_type=f32)
        s_b = lax.dot_general(q, k_ref[:own, :], nt, preferred_element_type=f32)
        s_a = s_a * scale + bias[i, :, :cut]
        s_b = s_b * scale + bias[i, :, cut:]
        top = jnp.maximum(
            jnp.max(s_a, axis=-1, keepdims=True), jnp.max(s_b, axis=-1, keepdims=True)
        )
        e_a = jnp.exp(s_a - top)
        e_b = jnp.exp(s_b - top)
        inv = 1.0 / (
            jnp.sum(e_a, axis=-1, keepdims=True) + jnp.sum(e_b, axis=-1, keepdims=True)
        )
        mixed = jnp.dot((e_a * inv).astype(bf16), pv_ref[first:, :], preferred_element_type=f32)
        mixed += jnp.dot((e_b * inv).astype(bf16), v_ref[:own, :], preferred_element_type=f32)
        o_ref[first : first + QB, :] = mixed.astype(bf16)


def attend(q_docs, k_docs, q, pk, k, pv, v):
    rows, width = q.shape
    col = pl.BlockSpec((rows, HD), lambda h: (0, h))
    return pl.pallas_call(
        attend_kernel,
        grid=(width // HD,),
        in_specs=[
            pl.BlockSpec((rows, 1), lambda h: (0, 0)),
            pl.BlockSpec((1, rows + WIN), lambda h: (0, 0)),
            col, col, col, col, col,
        ],
        out_specs=col,
        out_shape=jax.ShapeDtypeStruct((rows, width), bf16),
        scratch_shapes=[pltpu.VMEM((rows // QB, QB, WIN + QB), f32)],
        compiler_params=params(),
        cost_estimate=cost(16e9, 6 * MIB),
    )(q_docs, k_docs, q, pk, k, pv, v)


def pool_kernel(mine, other, w_mine, w_other, bytes_ref, ids, enc, sums, lead):
    half = bytes_ref.shape[0] // 2
    for i in range(2):
        part = slice(i * half, (i + 1) * half)
        term = jnp.dot(mine[part, :], w_mine[...], preferred_element_type=f32)
        term += jnp.dot(other[part, :], w_other[...], preferred_element_type=f32)
        enc[part, :] = (bytes_ref[part, :].astype(f32) + term).astype(bf16)
    rows = bytes_ref.shape[0]
    slot = lax.broadcasted_iota(jnp.int32, (CAP, rows), 0)
    member = (ids[...] == slot).astype(f32).astype(bf16)
    sums[...] = jnp.dot(member, enc[...], preferred_element_type=f32)
    leading = jnp.broadcast_to((ids[...] < 0).astype(f32), (8, rows))
    count = jnp.sum(leading, axis=1, keepdims=True)
    total = jnp.dot(leading.astype(bf16), enc[...], preferred_element_type=f32)
    at = lax.broadcasted_iota(jnp.int32, total.shape, 0)
    lead[...] = jnp.where(at == 1, count, total)


def pool(mine, other, w_mine, w_other, byte_states, ids_row):
    rows, width = byte_states.shape
    return pl.pallas_call(
        pool_kernel,
        in_specs=[VM] * 6,
        out_specs=[VM] * 3,
        out_shape=[
            jax.ShapeDtypeStruct((rows, width), bf16),
            jax.ShapeDtypeStruct((CAP, width), f32),
            jax.ShapeDtypeStruct((8, width), f32),
        ],
        compiler_params=params(),
        cost_estimate=cost(4e9, 10 * MIB),
    )(mine, other, w_mine, w_other, byte_states, ids_row)


def main_kernel(n_pairs, sources, gn, *refs):
    gus, dns = refs[:n_pairs], refs[n_pairs : 2 * n_pairs]
    keep, send, wg, wu, wd, hid, sem_g, sem_u, sem_d = refs[2 * n_pairs :]
    depth = wg.shape[0] // (2 * n_pairs)
    s = lax.axis_index("seq")
    h = lax.axis_index("head")
    copies_g, copies_u, copies_d = [], [], []
    for j in range(n_pairs):
        for m in range(2):
            if sources is None:
                place = (2 * j + m) * depth
            else:
                index = s
                for bit in sources[j][m]:
                    index = flip(index, bit)
                place = pl.multiple_of(index * depth, depth)
            rows = pl.ds(m * depth, depth)
            at = 2 * j + m
            copies_g.append(pltpu.make_async_copy(
                gus[j].at[0, rows], wg.at[pl.ds(place, depth)], sem_g.at[at]))
            copies_u.append(pltpu.make_async_copy(
                gus[j].at[1, rows], wu.at[pl.ds(place, depth)], sem_u.at[at]))
            copies_d.append(pltpu.make_async_copy(
                dns[j].at[m], wd.at[:, pl.ds(place, depth)], sem_d.at[at]))
    for copy in copies_g + copies_u + copies_d:
        copy.start()
    for copy in copies_g + copies_u:
        copy.wait()
    units = wg.shape[1]
    tile = 384
    for t in range(units // tile):
        cols = slice(t * tile, (t + 1) * tile)
        gate = jnp.dot(gn[...], wg[:, cols], preferred_element_type=f32)
        up = jnp.dot(gn[...], wu[:, cols], preferred_element_type=f32)
        hid[:, cols] = (jax.nn.silu(gate) * up).astype(bf16)
    for copy in copies_d:
        copy.wait()
    width = send.shape[1]
    step = 512
    for t in range(width // step):
        out = pl.ds(t * step, step)
        there = pl.ds(pl.multiple_of((1 - h) * width + t * step, step), step)
        send[:, out] = jnp.dot(hid[...], wd[:, there], preferred_element_type=f32).astype(bf16)
    for t in range(width // step):
        out = pl.ds(t * step, step)
        here = pl.ds(pl.multiple_of(h * width + t * step, step), step)
        keep[:, out] = jnp.dot(hid[...], wd[:, here], preferred_element_type=f32)


def main_layer(gn, gus, dns, sources):
    tokens, dm = gn.shape
    units = gus[0].shape[2]
    n_pairs = len(gus)
    n_blocks = 2 * n_pairs
    return pl.pallas_call(
        functools.partial(main_kernel, n_pairs, sources),
        in_specs=[VM] + [ANY] * (2 * n_pairs),
        out_specs=[VM, VM],
        out_shape=[
            jax.ShapeDtypeStruct((tokens, dm // 2), f32),
            jax.ShapeDtypeStruct((tokens, dm // 2), bf16),
        ],
        scratch_shapes=[
            pltpu.VMEM((dm, units), bf16),
            pltpu.VMEM((dm, units), bf16),
            pltpu.VMEM((units, dm), bf16),
            pltpu.VMEM((tokens, units), bf16),
            pltpu.SemaphoreType.DMA((n_blocks,)),
            pltpu.SemaphoreType.DMA((n_blocks,)),
            pltpu.SemaphoreType.DMA((n_blocks,)),
        ],
        compiler_params=params(),
        cost_estimate=cost(8e9, 20 * MIB),
    )(gn, *gus, *dns)


def back_kernel(starts, mine, other, w_back, back, tail):
    h = lax.axis_index("head")
    half = mine.shape[1]
    w_mine = w_back[pl.ds(pl.multiple_of(h * half, half), half), :]
    w_other = w_back[pl.ds(pl.multiple_of((1 - h) * half, half), half), :]
    total = jnp.dot(mine[...], w_mine, preferred_element_type=f32)
    total += jnp.dot(other[...], w_other, preferred_element_type=f32)
    back[...] = total.astype(bf16)
    row = lax.broadcasted_iota(jnp.int32, (16, CAP), 0)
    slot = lax.broadcasted_iota(jnp.int32, (16, CAP), 1)
    pick = (slot == starts[0] - 2 + row) & (row < 2)
    tail[...] = jnp.dot(
        pick.astype(f32).astype(bf16), back[...], preferred_element_type=f32
    ).astype(bf16)


def back_rows(starts, mine, other, w_back):
    width = w_back.shape[1]
    return pl.pallas_call(
        back_kernel,
        in_specs=[pl.BlockSpec(memory_space=pltpu.SMEM), VM, VM, VM],
        out_specs=[VM, VM],
        out_shape=[
            jax.ShapeDtypeStruct((mine.shape[0], width), bf16),
            jax.ShapeDtypeStruct((16, width), bf16),
        ],
        compiler_params=params(),
        cost_estimate=cost(3e9, 8 * MIB),
    )(starts, mine, other, w_back)


def lift_kernel(ids, enc, back, tail, out):
    group = ids[...]
    rows = group.shape[0]
    slot = lax.broadcasted_iota(jnp.int32, (rows, CAP), 1)
    pick = (group - 1 == slot).astype(f32).astype(bf16)
    lifted = jnp.dot(pick, back[...], preferred_element_type=f32)
    lifted += jnp.where(group == -1, tail[0:1, :].astype(f32), 0.0)
    lifted += jnp.where(group == 0, tail[1:2, :].astype(f32), 0.0)
    out[...] = (enc[...].astype(f32) + lifted).astype(bf16)


def lift(ids_col, encoded, back, tail):
    rows, width = encoded.shape
    block = 256
    return pl.pallas_call(
        lift_kernel,
        grid=(rows // block,),
        in_specs=[
            pl.BlockSpec((block, 1), lambda i: (i, 0)),
            pl.BlockSpec((block, width), lambda i: (i, 0)),
            pl.BlockSpec(back.shape, lambda i: (0, 0)),
            pl.BlockSpec(tail.shape, lambda i: (0, 0)),
        ],
        out_specs=pl.BlockSpec((block, width), lambda i: (i, 0)),
        out_shape=jax.ShapeDtypeStruct((rows, width), bf16),
        compiler_params=params(),
        cost_estimate=cost(2e9, 6 * MIB),
    )(ids_col, encoded, back, tail)


def gather_weights(w_gate, w_up, w_down, role):
    n_seq = lax.axis_size("seq")
    units = w_gate.shape[1] // 2
    depth = w_gate.shape[0]

    if n_seq != 16:
        mine = role * units
        gate = lax.dynamic_slice_in_dim(lax.all_gather(w_gate, "seq", axis=0, tiled=True), mine, units, 1)
        up = lax.dynamic_slice_in_dim(lax.all_gather(w_up, "seq", axis=0, tiled=True), mine, units, 1)
        down = lax.dynamic_slice_in_dim(lax.all_gather(w_down, "seq", axis=1, tiled=True), mine, units, 0)
        both = jnp.stack([gate, up])
        gus = [both[:, i : i + 256] for i in range(0, both.shape[1], 256)]
        dns = [
            jnp.stack([down[:, i : i + 128], down[:, i + 128 : i + 256]])
            for i in range(0, down.shape[1], 256)
        ]
        return gus, dns, None

    def half(of):
        return (
            jnp.stack([
                lax.dynamic_slice_in_dim(w_gate, of * units, units, 1),
                lax.dynamic_slice_in_dim(w_up, of * units, units, 1),
            ]),
            lax.dynamic_slice_in_dim(w_down, of * units, units, 0),
        )

    gu_mine, dn_mine = half(role)
    gu_theirs, dn_theirs = half(1 - role)
    gu = jnp.concatenate([gu_mine, swapped(gu_theirs, PAIR)], axis=1)
    dn = jnp.stack([dn_mine, swapped(dn_theirs, PAIR)])

    gu_z = swapped(gu, 8)
    gu_x, gu_y = swapped(gu, 1), swapped(gu, 2)
    dn_z = swapped(dn, 8)
    gu_xy = jnp.stack([swapped(gu_x[0], 2), swapped(gu_y[1], 1)])
    gu_zx, gu_zy = swapped(gu_z, 1), swapped(gu_z, 2)
    dn_x, dn_y = swapped(dn, 1), swapped(dn, 2)
    gu_zxy = jnp.stack([swapped(gu_zx[0], 2), swapped(gu_zy[1], 1)])
    dn_xy = swapped(dn_x, 2)
    dn_zx, dn_zy = swapped(dn_z, 1), swapped(dn_z, 2)
    dn_zxy = swapped(dn_zy, 1)
    gus = [gu, gu_z, gu_x, gu_y, gu_xy, gu_zx, gu_zy, gu_zxy]
    dns = [dn, dn_z, dn_x, dn_y, dn_xy, dn_zx, dn_zy, dn_zxy]
    ways = [(), (8,), (1,), (2,), (1, 2), (8, 1), (8, 2), (8, 1, 2)]
    sources = [(way, way + (PAIR,)) for way in ways]
    return gus, dns, sources


def by_head(mine, other, head, axis):
    low = jnp.where(head == 0, mine, other)
    high = jnp.where(head == 0, other, mine)
    return jnp.concatenate([low, high], axis=axis)


def body(byte_states, doc_ids, boundary_flags, w_qkv, w_out, w_span, w_gate, w_up, w_down, w_back):
    rows, width = byte_states.shape
    s = lax.axis_index("seq")
    head = lax.axis_index("head")
    role = (s // PAIR) % 2

    half = lax.dynamic_slice_in_dim(byte_states, head * (rows // 2), rows // 2, 0)
    prior_half = shifted(half, "seq", 1)
    prior_docs = jnp.where(s == 0, -1, shifted(doc_ids, "seq", 1))
    w_out_other = swapped(w_out, 1, "head")
    gus, dns, sources = gather_weights(w_gate, w_up, w_down, role)

    normed = rms_rows(byte_states.astype(f32)).astype(bf16)
    queries = jnp.dot(normed, w_qkv[0], preferred_element_type=f32).astype(bf16)
    keys = jnp.dot(normed, w_qkv[1], preferred_element_type=f32).astype(bf16)
    values = jnp.dot(normed, w_qkv[2], preferred_element_type=f32).astype(bf16)
    prior = by_head(prior_half, swapped(prior_half, 1, "head"), head, 0)
    prior_normed = rms_rows(prior.astype(f32)).astype(bf16)
    prior_keys = jnp.dot(prior_normed, w_qkv[1], preferred_element_type=f32).astype(bf16)
    prior_values = jnp.dot(prior_normed, w_qkv[2], preferred_element_type=f32).astype(bf16)

    all_docs = jnp.concatenate([prior_docs, doc_ids])
    attended = attend(
        doc_ids[:, None], all_docs[None, :], queries, prior_keys, keys, prior_values, values
    )
    attended_other = swapped(attended, 1, "head")

    local_ids = jnp.cumsum(boundary_flags, dtype=jnp.int32) - 1
    starts = jnp.sum(boundary_flags, dtype=jnp.int32)
    encoded, sums, lead = pool(
        attended, attended_other, w_out, w_out_other, byte_states, local_ids[None, :]
    )
    following = shifted(lead, "seq", -1)
    slots = jnp.arange(CAP, dtype=jnp.int32)
    counts = jnp.sum(local_ids[None, :] == slots[:, None], axis=1).astype(f32)
    last_slot = slots == starts - 1
    sums = sums + jnp.where(last_slot[:, None], following[0:1], f32(0.0))
    counts = counts + jnp.where(last_slot, following[1, 0], f32(0.0))
    pooled = (sums / jnp.maximum(counts, 1.0)[:, None]).astype(bf16)

    share = lax.dynamic_slice_in_dim(pooled, head * (width // 2), width // 2, 1)
    got = swapped(share, PAIR)
    pooled_partner = by_head(got, swapped(got, 1, "head"), head, 1)

    def enter(values):
        group_in = jnp.dot(values, w_span, preferred_element_type=f32).astype(bf16)
        return group_in, rms_rows(group_in.astype(f32)).astype(bf16)

    group_in, group_normed = enter(pooled)
    _, partner_normed = enter(pooled_partner)
    keep_p, send_p = main_layer(partner_normed, gus, dns, sources)
    partner_sum = (keep_p + swapped(send_p, 1, "head").astype(f32)).astype(bf16)
    from_partner = swapped(partner_sum, PAIR)
    group_normed, partner_sum = lax.optimization_barrier((group_normed, partner_sum))
    keep, send = main_layer(group_normed, gus, dns, sources)
    piece = send.shape[0] // 2
    arrived = [
        swapped(send[i * piece : (i + 1) * piece], 1, "head").astype(f32) for i in range(2)
    ]
    own_sum = keep + jnp.concatenate(arrived)
    own_sum, from_partner = lax.optimization_barrier((own_sum, from_partner))
    dm_half = keep.shape[1]
    in_half = lax.dynamic_slice_in_dim(group_in, head * dm_half, dm_half, 1)
    main = (in_half.astype(f32) + own_sum + from_partner.astype(f32)).astype(bf16)
    main_other = swapped(main, 1, "head")
    back, tail = back_rows(starts[None], main, main_other, w_back)
    prior_tail = shifted(tail, "seq", 1)
    return lift(local_ids[:, None], encoded, back, prior_tail)


def solution(mesh):
    placed = (
        P("seq", None),
        P("seq"),
        P("seq"),
        P(None, None, "head"),
        P("head", None),
        P(),
        P("seq", "head"),
        P("seq", "head"),
        P("head", "seq"),
        P(),
    )
    return jax.shard_map(
        body, mesh=mesh, in_specs=placed, out_specs=P("seq", None), check_vma=False
    )
```
